256 devices in a mesh: ka: 64 (over y, x, z_lo), ga: 4 (over z_hi, core).
Axes of the slice: x: 4, y: 4, z: 8 (z_hi: 2, z_lo: 4; z = z_hi * 4 + z_lo), core: 2. Of those that a mesh axis runs over, the one named last changes fastest.
Arguments:
- density: bfloat16 [128, 2, 64, 1024], P('ka', None, None, 'ga'), may hold values from -1.75 to 1.75
- partner: int32 [128], replicated, may hold values from 0 to 127, as said below
- qindex: int32 [128, 128], P('ka'), may hold values from 0 to 7
- gshift: int32 [128, 1024], P('ka'), may hold values from 0 to 1023, each once within a row
- screened: bfloat16 [8, 2, 1024, 1024], P(None, None, None, 'ga'), may hold values from -0.1875 to 0.1875
- coulomb: float32 [1024], P('ga'), may hold values from 0.25 to 2
Outputs:
- coupling: bfloat16 [128, 128, 2, 4096], P('ga', 'ka')
The draws below stay inside these ranges and needn't reach their ends.
Inputs may be any that keep to these rules, and one draw needn't show every extreme that they name: partner[partner[k]] = k and partner[k] != k.
All inputs are finite; a program needn't handle non-finite values.
Results may differ from the reference program's by a relative error of at most 0.0049.
Values may be sent and summed in bfloat16 or wider, within the bound.
A program may use at most 128 MiB of HBM per device.

```python
import math
import jax
import jax.numpy as jnp
from jax import lax

PAIRS = 64
NG = 1024
NQ = 8
NKR = 128


def draw_partner(key, part):
    key = jax.random.fold_in(key, 7)
    order = jax.random.permutation(key, NKR).astype(jnp.int32)
    firsts = order[0::2]
    seconds = order[1::2]
    result = jnp.zeros((NKR,), jnp.int32)
    result = result.at[firsts].set(seconds)
    result = result.at[seconds].set(firsts)
    return result


def set_ends(values, own_key, low, high):
    dims = values.shape
    spot = [jax.random.randint(jax.random.fold_in(own_key, axis), (), 0, dims[axis]) for axis in range(len(dims))]
    values = values.at[tuple(spot)].set(low)
    longest = dims.index(max(dims))
    spot[longest] = (spot[longest] + 1) % dims[longest]
    return values.at[tuple(spot)].set(high)


def with_spikes(values, stream_key, source, target, blocks, factor):
    def block_of(position):
        return (jnp.arange(values.shape[position]) // (values.shape[position] // blocks)).reshape((-1,) + (1,) * (values.ndim - 1 - position))

    first = jax.random.permutation(stream_key, blocks)[block_of(target)]
    second = (block_of(target) + blocks // 2) % blocks
    return jnp.where((block_of(source) == first) | (block_of(source) == second), factor * values, values)


def steps_of(stream_key, shape, pieces, low, high):
    level, own = 1.0, jax.random.fold_in(stream_key, 6)
    for position, shards_of in pieces:
        draws = jnp.exp(jax.random.uniform(jax.random.fold_in(own, position), (shards_of,), jnp.float32, low / len(pieces), high / len(pieces)))
        level = level * jnp.repeat(draws, shape[position] // shards_of).reshape([-1 if axis == position else 1 for axis in range(len(shape))])
    return level


def gaussian(own_key, shape, deviation, limit, shards=(), dtype=jnp.bfloat16):
    gain = steps_of(own_key, shape, shards, -0.22, 0.18) if shards else 1.0
    values = jax.random.normal(own_key, shape, jnp.float32) * deviation * gain
    return jnp.minimum(jnp.maximum(values, -limit), limit).astype(dtype)


def heavy_noise(stream_key, extent, deviation, limit, split, heavy, kind=jnp.bfloat16):
    array = deviation * jax.random.normal(stream_key, extent, jnp.float32)
    if split:
        array = array * steps_of(stream_key, extent, split, -0.22, 0.18)
    return jnp.clip(with_spikes(array, jax.random.fold_in(stream_key, 3), *heavy), -limit, limit).astype(kind)


def setup_inputs(seed: int = 0) -> dict:
    seeds = jax.random.split(jax.random.key(seed), 7)
    return {
        "density": heavy_noise(seeds[0], (NKR, 2, PAIRS, NG), 0.1, 1.75, ((0, 64), (3, 4)), (3, 0, 64, 4.0)),
        "partner": draw_partner(jax.random.fold_in(seeds[6], 71), 0),
        "qindex": set_ends(jax.random.randint(seeds[2], (NKR, NKR), 0, NQ), jax.random.fold_in(seeds[2], 1), 0, NQ - 1).astype(jnp.int32),
        "gshift": jax.vmap(lambda own: jax.random.permutation(own, NG))(jax.random.split(seeds[3], NKR)).reshape((NKR, NG)).astype(jnp.int32),
        "screened": gaussian(seeds[4], (NQ, 2, NG, NG), NG ** -0.5, 0.1875, ((3, 4),)),
        "coulomb": jnp.clip(jnp.exp(math.log(2.0) - 2.0794415 * jax.random.uniform(seeds[5], (NG,), jnp.float32) ** steps_of(seeds[5], (NG,), ((0, 4),), -0.2, 0.2)), 0.25, 2.0),
    }


def reference(density, partner, qindex, gshift, screened, coulomb):
    picked = density[partner]
    tilde = jnp.concatenate([picked[:, :1], -picked[:, 1:]], axis=1).astype(jnp.bfloat16)
    tilde_f = tilde.astype(jnp.float32)
    weights = screened.astype(jnp.float32)

    def one_row(items):
        row, qrow, srow = items
        shifted = jnp.take(row, srow, axis=2).astype(jnp.float32)
        prod = jnp.einsum('cpg,qdgh->qcdph', shifted, weights)
        x_re = prod[:, 0, 0] - prod[:, 1, 1]
        x_im = prod[:, 0, 1] + prod[:, 1, 0]
        product = jnp.stack([x_re, x_im], axis=1)
        kernel = (2.0 * coulomb * shifted[None] - product).astype(jnp.bfloat16)
        chosen = jnp.take(kernel, qrow, axis=0).astype(jnp.float32)
        block = jnp.einsum('jcpg,jdrg->jcdpr', chosen, tilde_f)
        b_re = block[:, 0, 0] - block[:, 1, 1]
        b_im = block[:, 0, 1] + block[:, 1, 0]
        return jnp.stack([b_re, b_im], axis=1).reshape(NKR, 2, PAIRS * PAIRS)

    rows_out = lax.map(one_row, (density, qindex, gshift))
    return jnp.swapaxes(rows_out, 0, 1).astype(jnp.bfloat16)
```

```python
import functools

import jax
import jax.numpy as jnp
from jax import lax
from jax.experimental import pallas as pl
from jax.experimental.pallas import tpu as pltpu
from jax.sharding import PartitionSpec as P

MESH = pl.DeviceIdType.MESH
F32, BF16 = jnp.float32, jnp.bfloat16
PAIRS, NG, NQ, NKR, WIDTH = 64, 1024, 8, 128, 256
CHUNKS = 8
RC = PAIRS // CHUNKS
BLOCK = NKR // 4
GROUPS = ((0, 1), (1, 3), (3, 8))
NT = (((1,), (1,)), ((), ()))


def dot(a, b):
    return jnp.dot(a, b, preferred_element_type=F32)


def dot_nt(a, b):
    return lax.dot_general(a, b, NT, preferred_element_type=F32)


def kernel(density, partner, qindex, gshift, screened, coulomb, out,
           D, SG, OH, SH, W, KA, KB, res, xsend, xrecv, keepx, fin, csend, crecv,
           wsem, s_s, s_r, z_s, z_r, a1_s, a1_r, a2_s, a2_r, b1_s, b1_r, b2_s, b2_r, x_s, x_r, c_s, c_r):
    ka, ga = lax.axis_index("ka"), lax.axis_index("ga")
    y, x, z = ka // 16, (ka // 4) % 4, ka % 4
    half, core = ga // 2, ga % 2
    ym, yp, yo = (y + 3) % 4, (y + 1) % 4, (y + 2) % 4
    xm, xp, xo = (x + 3) % 4, (x + 1) % 4, (x + 2) % 4

    def at(yy, xx, zz):
        return (yy * 16 + xx * 4 + zz, ga)

    mate_ga = half * 2 + (1 - core)
    cross_ga = (1 - half) * 2 + core
    far_ga = (1 - half) * 2 + (1 - core)
    mate, cross = (ka, mate_ga), (ka, cross_ga)
    line = [at(y, x, (z + d) % 4) for d in (1, 2, 3)]
    ring = [at(y, xp, z), at(y, xm, z), at(yp, x, z), at(ym, x, z)]
    ring_b = [ring[2], ring[3], ring[0], ring[1]]

    def rc(src, dst, ss, rs, dev):
        return pltpu.make_async_remote_copy(
            src_ref=src, dst_ref=dst, send_sem=ss, recv_sem=rs, device_id=dev, device_id_type=MESH)

    def got(land, ss, rs, dev):
        rc(land, land, ss, rs, dev).wait_recv()

    def sent(src, ss, rs, dev):
        rc(src, src, ss, rs, dev).wait_send()

    barrier = pltpu.get_barrier_semaphore()
    for peer in line + ring + [mate, cross]:
        pl.semaphore_signal(barrier, inc=1, device_id=peer, device_id_type=MESH)
    wcopy = pltpu.make_async_copy(screened, W, wsem)
    wcopy.start()

    for h in range(2):
        both = [density[j, h].astype(F32).reshape(CHUNKS, RC, WIDTH) for j in range(2)]
        D[h, :, y, x, z] = jnp.concatenate(both, axis=1).astype(BF16)
    SG[ga] = density[...]
    pl.semaphore_wait(barrier, 9)

    s_parts = [(SG.at[ga], mate), (SG.at[ga], cross), (SG.at[cross_ga], mate)]
    s_land = [SG.at[mate_ga], SG.at[cross_ga], SG.at[far_ga]]

    def s_send(i):
        rc(s_parts[i][0], s_parts[i][0], s_s.at[i], s_r.at[i], s_parts[i][1]).start()

    def s_got(i):
        got(s_land[i], s_s.at[i], s_r.at[i], s_parts[i][1])

    def z_part(g, zz):
        lo, hi = GROUPS[g]
        return D.at[:, lo:hi, y, x, zz]

    def z_send(g):
        for d in range(3):
            rc(z_part(g, z), z_part(g, z), z_s.at[g, d], z_r.at[g, d], line[d]).start()

    def z_got(g):
        for d in range(3):
            got(z_part(g, (z + 3 - d) % 4), z_s.at[g, d], z_r.at[g, d], line[d])

    def a1_src(c):
        return [D.at[0, c, y, x], D.at[0, c, y, x], D.at[1, c, y, x], D.at[1, c, y, x]]

    def a1_land(c):
        return [D.at[0, c, y, xm], D.at[0, c, y, xp], D.at[1, c, ym, x], D.at[1, c, yp, x]]

    def a2_src(c):
        return [D.at[0, c, y, xm, 0:2], D.at[0, c, y, xp, 2:4], D.at[1, c, ym, x, 0:2], D.at[1, c, yp, x, 2:4]]

    def a2_land(c):
        return [D.at[0, c, y, xo, 0:2], D.at[0, c, y, xo, 2:4], D.at[1, c, yo, x, 0:2], D.at[1, c, yo, x, 2:4]]

    def b1_src(c):
        return [D.at[0, c, y], D.at[0, c, y], D.at[1, c, :, x], D.at[1, c, :, x]]

    def b1_land(c):
        return [D.at[0, c, ym], D.at[0, c, yp], D.at[1, c, :, xm], D.at[1, c, :, xp]]

    def b2_src(c):
        return [D.at[0, c, ym, 0:2], D.at[0, c, yp, 2:4], D.at[1, c, 0:2, xm], D.at[1, c, 2:4, xp]]

    def b2_land(c):
        return [D.at[0, c, yo, 0:2], D.at[0, c, yo, 2:4], D.at[1, c, 0:2, xo], D.at[1, c, 2:4, xo]]

    phases = {
        "a1": (a1_src, a1_land, a1_s, a1_r, ring),
        "a2": (a2_src, a2_land, a2_s, a2_r, ring),
        "b1": (b1_src, b1_land, b1_s, b1_r, ring_b),
        "b2": (b2_src, b2_land, b2_s, b2_r, ring_b),
    }

    def send(name, c):
        src, _, ss, rs, to = phases[name]
        for i, part in enumerate(src(c)):
            rc(part, part, ss.at[c, i], rs.at[c, i], to[i]).start()

    def recv(name, c):
        _, land, ss, rs, to = phases[name]
        for i, part in enumerate(land(c)):
            got(part, ss.at[c, i], rs.at[c, i], to[i])

    def done(name, c):
        src, _, ss, rs, to = phases[name]
        for i, part in enumerate(src(c)):
            sent(part, ss.at[c, i], rs.at[c, i], to[i])

    def shift_part(b, first):
        rows = pl.ds(pl.multiple_of(b * WIDTH, WIDTH), WIDTH)
        for j in range(2):
            term = dot(SG[b, j].reshape(2 * PAIRS, WIDTH), OH[j, rows, :])
            if first:
                SH[j] = term.astype(BF16)
            else:
                SH[j] = (SH[j].astype(F32) + term).astype(BF16)

    s_send(1)
    s_send(0)
    z_send(0)

    def build(t, _):
        rows = pl.ds(pl.multiple_of(t * 64, 64), 64)
        index = lax.broadcasted_iota(jnp.int32, (64, NG), 0) + t * 64
        for j in range(2):
            OH[j, rows, :] = jnp.where(index == gshift[j:j + 1, :], 1.0, 0.0).astype(BF16)
        return 0

    lax.fori_loop(0, NG // 64, build, 0)

    z_got(0)
    send("a1", 0)
    z_send(1)
    recv("a1", 0)
    send("a2", 0)
    z_send(2)
    s_got(0)
    shift_part(ga, True)
    shift_part(mate_ga, False)
    recv("a2", 0)
    send("b1", 0)
    z_got(1)
    send("a1", 1)
    send("a1", 2)
    s_got(1)
    s_send(2)
    shift_part(cross_ga, False)
    recv("a1", 1)
    send("a2", 1)
    recv("b1", 0)
    send("b2", 0)
    recv("a1", 2)
    send("a2", 2)
    recv("a2", 1)
    send("b1", 1)
    z_got(2)
    send("a1", 3)
    s_got(2)
    shift_part(far_ga, False)
    wcopy.wait()

    local = pl.ds(pl.multiple_of(ga * WIDTH, WIDTH), WIDTH)

    def screen(q, _):
        rows = SH[...].reshape(4 * PAIRS, NG)
        by_re, by_im = dot(rows, W[q, 0]), dot(rows, W[q, 1])
        twice = 2.0 * coulomb[...]
        a, b = [], []
        for j in range(2):
            re, im = slice(j * 128, j * 128 + 64), slice(j * 128 + 64, j * 128 + 128)
            own = SH[j, :, local].astype(F32)
            k_re = (twice * own[:64] - (by_re[re] - by_im[im])).astype(BF16)
            k_im = (twice * own[64:] - (by_im[re] + by_re[im])).astype(BF16)
            a += [k_re, k_im]
            b += [k_im, -k_re]
        KA[q] = jnp.concatenate(a, axis=0)
        KB[q] = jnp.concatenate(b, axis=0)
        return 0

    lax.fori_loop(0, NQ, screen, 0)

    def multiply(c, q_lo, q_hi):
        def one(q, _):
            for t in range(4):
                d_re = D[0, c, t].reshape(256, WIDTH)
                d_im = D[1, c, t].reshape(256, WIDTH)
                both = dot_nt(d_re, KA[q]) + dot_nt(d_im, KB[q])
                for k in range(2):
                    res[k, q, t * 32:(t + 1) * 32] = both[:, k * 128:(k + 1) * 128].reshape(32, RC, 128)
            return 0

        lax.fori_loop(q_lo, q_hi, one, 0)

    def pick(block, put):
        def one(i, _):
            col = block * BLOCK + i
            m = partner[col]
            for k in range(2):
                put(i, k, res[k, qindex[k, col], m])
            return 0

        lax.fori_loop(0, BLOCK, one, 0, unroll=4)

    def x_send(c, part):
        rc(xsend.at[c, part], xrecv.at[c, part], x_s.at[c, part], x_r.at[c, part], mate).start()

    def x_got(c, part):
        got(xrecv.at[c, part], x_s.at[c, part], x_r.at[c, part], mate)

    def settle(c):
        def put_far(i, k, v):
            xsend[c, 0, i, k] = v

        def put_mate(i, k, v):
            xsend[c, 1, i, k] = v

        def put_cross(i, k, v):
            keepx[i, k] = v

        def put_own(i, k, v):
            fin[c, i, k] = v

        pick(far_ga, put_far)
        x_send(c, 0)
        pick(mate_ga, put_mate)
        x_send(c, 1)
        pick(cross_ga, put_cross)
        pick(ga, put_own)
        x_got(c, 0)
        total = keepx[...] + xrecv[c, 0]
        csend[c] = total.reshape(BLOCK, 2 * RC, 128).astype(BF16)
        rc(csend.at[c], crecv.at[c], c_s.at[c], c_r.at[c], cross).start()
        x_got(c, 1)
        fin[c] = fin[c] + xrecv[c, 1]

    def finish(c):
        got(crecv.at[c], c_s.at[c], c_r.at[c], cross)
        total = fin[c].reshape(BLOCK, 2 * RC, 128) + crecv[c].astype(F32)
        out[:, c] = total.astype(BF16)

    def tick(c, _):
        @pl.when(c + 2 < CHUNKS)
        def _():
            recv("a2", c + 2)
            send("b1", c + 2)

        recv("b2", c)
        multiply(c, 0, NQ // 2)

        @pl.when(c + 1 < CHUNKS)
        def _():
            recv("b1", c + 1)
            send("b2", c + 1)

        @pl.when(c + 3 < CHUNKS)
        def _():
            recv("a1", c + 3)
            send("a2", c + 3)

        @pl.when(c + 4 < CHUNKS)
        def _():
            send("a1", c + 4)

        multiply(c, NQ // 2, NQ)
        settle(c)

        @pl.when(c >= 3)
        def _():
            finish(c - 3)

        return 0

    lax.fori_loop(0, CHUNKS, tick, 0)

    def last(c, _):
        for name in phases:
            done(name, c)
        for part in range(2):
            sent(xsend.at[c, part], x_s.at[c, part], x_r.at[c, part], mate)
        sent(csend.at[c], c_s.at[c], c_r.at[c], cross)
        return 0

    lax.fori_loop(0, CHUNKS, last, 0)
    for i in range(3):
        sent(s_parts[i][0], s_s.at[i], s_r.at[i], s_parts[i][1])
    for g in range(3):
        for d in range(3):
            sent(z_part(g, z), z_s.at[g, d], z_r.at[g, d], line[d])
    for c in range(CHUNKS - 3, CHUNKS):
        finish(c)


def on_device(density, partner, qindex, gshift, screened, coulomb):
    vmem = pl.BlockSpec(memory_space=pltpu.VMEM)
    smem = pl.BlockSpec(memory_space=pltpu.SMEM)
    dma = pltpu.SemaphoreType.DMA
    ring_sems = [dma((CHUNKS, 4))] * 8
    packed = pl.pallas_call(
        kernel,
        out_shape=jax.ShapeDtypeStruct((BLOCK, CHUNKS, 2 * RC, 128), BF16),
        in_specs=[vmem, smem, smem, vmem, pl.BlockSpec(memory_space=pl.ANY), vmem],
        out_specs=vmem,
        scratch_shapes=[
            pltpu.VMEM((2, CHUNKS, 4, 4, 4, 2 * RC, WIDTH), BF16),
            pltpu.VMEM((4, 2, 2, PAIRS, WIDTH), BF16),
            pltpu.VMEM((2, NG, NG), BF16),
            pltpu.VMEM((2, 2 * PAIRS, NG), BF16),
            pltpu.VMEM((NQ, 2, NG, WIDTH), BF16),
            pltpu.VMEM((NQ, 4 * PAIRS, WIDTH), BF16),
            pltpu.VMEM((NQ, 4 * PAIRS, WIDTH), BF16),
            pltpu.VMEM((2, NQ, NKR, RC, 128), F32),
            pltpu.VMEM((CHUNKS, 2, BLOCK, 2, RC, 128), F32),
            pltpu.VMEM((CHUNKS, 2, BLOCK, 2, RC, 128), F32),
            pltpu.VMEM((BLOCK, 2, RC, 128), F32),
            pltpu.VMEM((CHUNKS, BLOCK, 2, RC, 128), F32),
            pltpu.VMEM((CHUNKS, BLOCK, 2 * RC, 128), BF16),
            pltpu.VMEM((CHUNKS, BLOCK, 2 * RC, 128), BF16),
            dma, dma((3,)), dma((3,)), dma((3, 3)), dma((3, 3)),
        ] + ring_sems + [dma((CHUNKS, 2)), dma((CHUNKS, 2)), dma((CHUNKS,)), dma((CHUNKS,))],
        compiler_params=pltpu.CompilerParams(
            collective_id=0, has_side_effects=True, vmem_limit_bytes=56 << 20),
    )(density, partner, qindex, gshift, screened, coulomb.reshape(1, WIDTH))
    parts = packed.reshape(BLOCK, CHUNKS, 2, RC, 2, PAIRS)
    return parts.transpose(0, 2, 4, 5, 1, 3).reshape(BLOCK, 2, 2, PAIRS * PAIRS)


def solution(mesh):
    return jax.shard_map(
        on_device,
        mesh=mesh,
        in_specs=(
            P("ka", None, None, "ga"),
            P(),
            P("ka", None),
            P("ka", None),
            P(None, None, None, "ga"),
            P("ga"),
        ),
        out_specs=P("ga", "ka", None, None),
        check_vma=False,
    )
```

```python
import functools

import jax
import jax.numpy as jnp
from jax import lax
from jax.experimental import pallas as pl
from jax.experimental.pallas import tpu as pltpu
from jax.sharding import PartitionSpec as P

MESH = pl.DeviceIdType.MESH
F32, BF16 = jnp.float32, jnp.bfloat16
PAIRS, NG, NQ, NKR, WIDTH = 64, 1024, 8, 128, 256
CHUNKS = 8
RC = PAIRS // CHUNKS
BLOCK = NKR // 4
GROUPS = ((0, 2), (2, 4), (4, 6), (6, 8))
DIRECT = 1
SLABS = 4
SLAB = BLOCK // SLABS
NT = (((1,), (1,)), ((), ()))


def dot(a, b):
    return jnp.dot(a, b, preferred_element_type=F32)


def dot_nt(a, b):
    return lax.dot_general(a, b, NT, preferred_element_type=F32)


def kernel(density, partner, qindex, gshift, screened, coulomb, out,
           D, SG, OH, SH, W, KA, KB, res, xsend, xrecv, keepx, fin, csend, crecv, obuf,
           wsem, out_sem, s_r, z_r, a1_r, a2_r, b1_r, b2_r, x_r, c_r, l_r, osem):
    ka, ga = lax.axis_index("ka"), lax.axis_index("ga")
    y, x, z = ka // 16, (ka // 4) % 4, ka % 4
    half, core = ga // 2, ga % 2
    ym, yp, yo = (y + 3) % 4, (y + 1) % 4, (y + 2) % 4
    xm, xp, xo = (x + 3) % 4, (x + 1) % 4, (x + 2) % 4

    def at(yy, xx, zz):
        return (yy * 16 + xx * 4 + zz, ga)

    mate_ga = half * 2 + (1 - core)
    cross_ga = (1 - half) * 2 + core
    far_ga = (1 - half) * 2 + (1 - core)
    mate, cross = (ka, mate_ga), (ka, cross_ga)
    line = [at(y, x, (z + d) % 4) for d in (1, 2, 3)]
    ring = [at(y, xp, z), at(y, xm, z), at(yp, x, z), at(ym, x, z)]
    ring_b = [ring[2], ring[3], ring[0], ring[1]]
    opposite = [at(y, xo, z), at(yo, x, z)]

    def rc(src, dst, ss, rs, dev):
        return pltpu.make_async_remote_copy(
            src_ref=src, dst_ref=dst, send_sem=ss, recv_sem=rs, device_id=dev, device_id_type=MESH)

    z_s, a1_s, a2_s, b1_s, b2_s, s_s, x_s, c_s = (out_sem.at[i] for i in range(8))

    def got(whole, rs):
        rc(whole, whole, z_s, rs, mate).wait_recv()

    def sent(whole, ss):
        rc(whole, whole, ss, s_r.at[0], mate).wait_send()

    barrier = pltpu.get_barrier_semaphore()
    for peer in line + ring + opposite + [mate, cross]:
        pl.semaphore_signal(barrier, inc=1, device_id=peer, device_id_type=MESH)
    wcopy = pltpu.make_async_copy(screened, W, wsem)
    wcopy.start()

    for h in range(2):
        both = [density[j, h].astype(F32).reshape(CHUNKS, RC, WIDTH) for j in range(2)]
        D[h, :, y, x, z] = jnp.concatenate(both, axis=1).astype(BF16)
    SG[ga] = density[...]
    pl.semaphore_wait(barrier, 11)

    s_parts = [(SG.at[ga], mate), (SG.at[ga], cross), (SG.at[cross_ga], mate)]
    s_land = [SG.at[mate_ga], SG.at[cross_ga], SG.at[far_ga]]

    def s_send(i):
        rc(s_parts[i][0], s_parts[i][0], s_s, s_r.at[i], s_parts[i][1]).start()

    def s_got(i):
        got(s_land[i], s_r.at[i])

    def z_send(g):
        lo, hi = GROUPS[g]
        part = D.at[:, lo:hi, y, x, z]
        for d in range(3):
            rc(part, part, z_s, z_r.at[g], line[d]).start()

    def z_got(g):
        lo, hi = GROUPS[g]
        got(D.at[:, lo:hi, 0, 0, 0:3], z_r.at[g])

    def span(g):
        return pl.ds(GROUPS[g][0], GROUPS[g][1] - GROUPS[g][0])

    def send_all(parts, ss, rs, to):
        for part, dev in zip(parts, to):
            rc(part, part, ss, rs, dev).start()


    def send(name, c):
        if name == "a1":
            w = span(c)
            parts = [D.at[0, w, y, x], D.at[0, w, y, x], D.at[1, w, y, x], D.at[1, w, y, x]]
            send_all(parts, a1_s, a1_r.at[c], ring)
            if c == 0:
                send_all(parts[1:3], z_s, a1_r.at[c], opposite)
        if name == "a2":
            w = span(c)
            parts = [D.at[0, w, y, xm, 0:2], D.at[0, w, y, xp, 2:4], D.at[1, w, ym, x, 0:2], D.at[1, w, yp, x, 2:4]]
            send_all(parts, a2_s, a2_r.at[c], ring)
        if name == "b1":
            parts = [D.at[0, c, y], D.at[0, c, y], D.at[1, c, :, x], D.at[1, c, :, x]]
            send_all(parts, b1_s, b1_r.at[c], ring_b)
            if isinstance(c, int) and c < DIRECT:
                send_all(parts[1:3], b2_s, b1_r.at[c], opposite[::-1])
        if name == "b2":
            parts = [D.at[0, c, ym, 0:2], D.at[0, c, yp, 2:4], D.at[1, c, 0:2, xm], D.at[1, c, 2:4, xp]]
            send_all(parts, b2_s, b2_r.at[c], ring_b)

    def recv(name, c):
        if name == "a1":
            got(D.at[:, span(c), 0, 0:3] if c == 0 else D.at[0, span(c), 0], a1_r.at[c])
        if name == "a2":
            got(D.at[0, span(c), 0, 0:2], a2_r.at[c])
        if name == "b1":
            got(D.at[:, c, 0:3] if isinstance(c, int) and c < DIRECT else D.at[0, c], b1_r.at[c])
        if name == "b2":
            got(D.at[0, c, 0:2], b2_r.at[c])

    def shift_part(b, first):
        rows = pl.ds(pl.multiple_of(b * WIDTH, WIDTH), WIDTH)
        for j in range(2):
            term = dot(SG[b, j].reshape(2 * PAIRS, WIDTH), OH[j, rows, :])
            if first:
                SH[j] = term.astype(BF16)
            else:
                SH[j] = (SH[j].astype(F32) + term).astype(BF16)

    z_send(0)

    def build(t, _):
        rows = pl.ds(pl.multiple_of(t * 64, 64), 64)
        index = lax.broadcasted_iota(jnp.int32, (64, NG), 0) + t * 64
        for j in range(2):
            OH[j, rows, :] = jnp.where(index == gshift[j:j + 1, :], 1.0, 0.0).astype(BF16)
        return 0

    lax.fori_loop(0, NG // 64, build, 0)
    s_send(1)
    s_send(0)
    shift_part(ga, True)

    local = pl.ds(pl.multiple_of(ga * WIDTH, WIDTH), WIDTH)

    def screen(q, _):
        rows = SH[...].reshape(4 * PAIRS, NG)
        by_re, by_im = dot(rows, W[q, 0]), dot(rows, W[q, 1])
        twice = 2.0 * coulomb[...]
        a, b = [], []
        for j in range(2):
            re, im = slice(j * 128, j * 128 + 64), slice(j * 128 + 64, j * 128 + 128)
            own = SH[j, :, local].astype(F32)
            k_re = (twice * own[:64] - (by_re[re] - by_im[im])).astype(BF16)
            k_im = (twice * own[64:] - (by_im[re] + by_re[im])).astype(BF16)
            a += [k_re, k_im]
            b += [k_im, -k_re]
        KA[q] = jnp.concatenate(a, axis=0)
        KB[q] = jnp.concatenate(b, axis=0)
        return 0

    local = pl.ds(pl.multiple_of(ga * WIDTH, WIDTH), WIDTH)

    def screen(q, _):
        rows = SH[...].reshape(4 * PAIRS, NG)
        by_re, by_im = dot(rows, W[q, 0]), dot(rows, W[q, 1])
        twice = 2.0 * coulomb[...]
        a, b = [], []
        for j in range(2):
            re, im = slice(j * 128, j * 128 + 64), slice(j * 128 + 64, j * 128 + 128)
            own = SH[j, :, local].astype(F32)
            k_re = (twice * own[:64] - (by_re[re] - by_im[im])).astype(BF16)
            k_im = (twice * own[64:] - (by_im[re] + by_re[im])).astype(BF16)
            a += [k_re, k_im]
            b += [k_im, -k_re]
        KA[q] = jnp.concatenate(a, axis=0)
        KB[q] = jnp.concatenate(b, axis=0)
        return 0

    z_got(0)
    send("a1", 0)
    s_got(0)
    shift_part(mate_ga, False)
    recv("a1", 0)
    send("b1", 0)
    s_got(1)
    s_send(2)
    send("b1", 1)
    z_send(1)
    z_send(2)
    z_send(3)
    shift_part(cross_ga, False)
    s_got(2)
    shift_part(far_ga, False)
    wcopy.wait()
    lax.fori_loop(0, 5, screen, 0)
    z_got(1)
    send("a1", 1)
    lax.fori_loop(5, NQ, screen, 0)

    def multiply(c, q_lo, q_hi):
        def one(q, _):
            for t in range(4):
                d_re = D[0, c, t].reshape(256, WIDTH)
                d_im = D[1, c, t].reshape(256, WIDTH)
                both = dot_nt(d_re, KA[q]) + dot_nt(d_im, KB[q])
                for k in range(2):
                    res[k, q, t * 32:(t + 1) * 32] = both[:, k * 128:(k + 1) * 128].reshape(32, RC, 128)
            return 0

        lax.fori_loop(q_lo, q_hi, one, 0)

    def pick(block, put):
        def one(i, _):
            col = block * BLOCK + i
            m = partner[col]
            for k in range(2):
                put(i, k, res[k, qindex[k, col], m])
            return 0

        lax.fori_loop(0, BLOCK, one, 0, unroll=4)

    def x_send(c, part):
        rc(xsend.at[c, part], xrecv.at[c, part], x_s, x_r.at[c, part], mate).start()

    def x_got(c, part):
        got(xrecv.at[c, part], x_r.at[c, part])

    def c_send(c):
        x_got(c, 0)
        for part in range(SLABS):
            piece = pl.ds(part * SLAB, SLAB)
            total = keepx[piece] + xrecv[c, 0, piece]
            csend[c, part] = total.reshape(SLAB, 2 * RC, 128).astype(BF16)
            arrived = l_r.at[part] if isinstance(c, int) and c == CHUNKS - 1 else c_r.at[c]
            rc(csend.at[c, part], crecv.at[c, part], c_s, arrived, cross).start()

    def settle(c):
        rows = pl.ds(pl.multiple_of(c * RC, RC), RC)

        def put_far(i, k, v):
            xsend[c, 0, i, k] = v

        def put_mate(i, k, v):
            xsend[c, 1, i, k] = v

        def put_cross(i, k, v):
            keepx[i, k] = v

        def put_own(i, k, v):
            fin[i, k, rows] = v

        pick(far_ga, put_far)
        x_send(c, 0)
        pick(cross_ga, put_cross)
        pick(mate_ga, put_mate)
        x_send(c, 1)
        pick(ga, put_own)

    def finish(c, part):
        rows = pl.ds(pl.multiple_of(c * RC, RC), RC)
        piece = pl.ds(part * SLAB, SLAB)
        theirs = crecv[c, part].astype(F32).reshape(SLAB, 2, RC, 128)
        fin[piece, :, rows] = fin[piece, :, rows] + xrecv[c, 1, piece] + theirs

    def turn(part):
        slot = lax.broadcasted_iota(jnp.int32, (PAIRS, 128), 0)
        pair = lax.broadcasted_iota(jnp.int32, (PAIRS, 128), 1)
        same = (slot % 2 == pair // PAIRS) & (slot // 2 == (pair % PAIRS) // 2)
        chosen = jnp.where(same, 1.0, 0.0).astype(BF16)
        even = pair % 2 == 0

        def one(i, _):
            parts = []
            for k in range(2):
                t = fin[i, k].astype(BF16)
                zero = jnp.zeros_like(t)
                parts += [jnp.where(even, t, zero), jnp.where(even, zero, t)]
            turned = dot_nt(chosen, jnp.concatenate(parts, axis=0)).astype(BF16)
            obuf[i, 0] = turned[:, :128]
            obuf[i, 1] = turned[:, 128:]
            return 0

        lax.fori_loop(part * SLAB, (part + 1) * SLAB, one, 0, unroll=4)

    def o_copy(part):
        piece = pl.ds(part * SLAB, SLAB)
        return pltpu.make_async_copy(obuf.at[piece], out.at[piece], osem.at[part])

    recv("b1", 0)
    multiply(0, 0, 2)
    recv("b1", 1)
    send("b2", 1)
    recv("a1", 1)
    send("a2", 1)
    z_got(2)
    send("a1", 2)
    multiply(0, 2, 6)
    recv("a2", 1)
    send("b1", 2)
    send("b1", 3)
    z_got(3)
    send("a1", 3)
    multiply(0, 6, NQ)
    settle(0)

    recv("b2", 1)
    multiply(1, 0, NQ // 2)
    c_send(0)
    recv("b1", 2)
    send("b2", 2)
    recv("a1", 2)
    send("a2", 2)
    multiply(1, NQ // 2, NQ)
    settle(1)
    recv("a2", 2)
    send("b1", 4)
    recv("a1", 3)
    send("a2", 3)

    def tick(c, _):
        @pl.when(c + 1 < CHUNKS)
        def _():
            recv("b1", c + 1)
            send("b2", c + 1)

        @pl.when(c == 3)
        def _():
            recv("a2", 3)

        @pl.when(c + 3 < CHUNKS)
        def _():
            send("b1", c + 3)

        recv("b2", c)
        multiply(c, 0, NQ // 2)
        c_send(c - 1)
        multiply(c, NQ // 2, NQ)
        settle(c)
        return 0

    lax.fori_loop(2, CHUNKS, tick, 0)
    c_send(CHUNKS - 1)

    def rest(c, _):
        x_got(c, 1)
        return 0

    lax.fori_loop(0, CHUNKS, rest, 0)
    sent(D.at[0, 0], z_s)
    sent(D.at[0, 0:2], a1_s)
    sent(D.at[0, 0, 0:3], a2_s)
    sent(D.at[0], b1_s)
    sent(D.at[0, 0:4], b2_s)
    sent(SG.at[0:3], s_s)
    sent(xsend, x_s)

    def ends(c, _):
        got(crecv.at[c], c_r.at[c])
        for part in range(SLABS):
            finish(c, part)
        return 0

    lax.fori_loop(0, CHUNKS - 1, ends, 0)
    for part in range(SLABS):
        got(crecv.at[CHUNKS - 1, part], l_r.at[part])
        finish(CHUNKS - 1, part)
        turn(part)
        o_copy(part).start()
    sent(csend, c_s)
    for part in range(SLABS):
        o_copy(part).wait()


def move(src, dst):
    dst[...] = src[...]


def on_device(density, partner, qindex, gshift, screened, coulomb):
    vmem = pl.BlockSpec(memory_space=pltpu.VMEM)
    smem = pl.BlockSpec(memory_space=pltpu.SMEM)
    dma = pltpu.SemaphoreType.DMA
    packed = pl.pallas_call(
        kernel,
        out_shape=jax.ShapeDtypeStruct((BLOCK, 2, PAIRS, 128), BF16),
        in_specs=[vmem, smem, smem, vmem, pl.BlockSpec(memory_space=pl.ANY), vmem],
        out_specs=pl.BlockSpec(memory_space=pl.ANY),
        scratch_shapes=[
            pltpu.VMEM((2, CHUNKS, 4, 4, 4, 2 * RC, WIDTH), BF16),
            pltpu.VMEM((4, 2, 2, PAIRS, WIDTH), BF16),
            pltpu.VMEM((2, NG, NG), BF16),
            pltpu.VMEM((2, 2 * PAIRS, NG), BF16),
            pltpu.VMEM((NQ, 2, NG, WIDTH), BF16),
            pltpu.VMEM((NQ, 4 * PAIRS, WIDTH), BF16),
            pltpu.VMEM((NQ, 4 * PAIRS, WIDTH), BF16),
            pltpu.VMEM((2, NQ, NKR, RC, 128), F32),
            pltpu.VMEM((CHUNKS, 2, BLOCK, 2, RC, 128), F32),
            pltpu.VMEM((CHUNKS, 2, BLOCK, 2, RC, 128), F32),
            pltpu.VMEM((BLOCK, 2, RC, 128), F32),
            pltpu.VMEM((BLOCK, 2, PAIRS, 128), F32),
            pltpu.VMEM((CHUNKS, SLABS, SLAB, 2 * RC, 128), BF16),
            pltpu.VMEM((CHUNKS, SLABS, SLAB, 2 * RC, 128), BF16),
            pltpu.VMEM((BLOCK, 2, PAIRS, 128), BF16),
            dma, dma((8,)), dma((3,)), dma((len(GROUPS),)), dma((len(GROUPS),)), dma((len(GROUPS),)),
            dma((CHUNKS,)), dma((CHUNKS,)), dma((CHUNKS, 2)), dma((CHUNKS,)), dma((SLABS,)), dma((SLABS,)),
        ],
        compiler_params=pltpu.CompilerParams(
            collective_id=0, has_side_effects=True, vmem_limit_bytes=56 << 20),
    )(density, partner, qindex, gshift, screened, coulomb.reshape(1, WIDTH))
    packed = pl.pallas_call(
        move,
        out_shape=jax.ShapeDtypeStruct(packed.shape, packed.dtype),
        in_specs=[vmem],
        out_specs=vmem,
    )(packed)
    rows = packed.reshape(BLOCK, 2, PAIRS // 2, 2, 2 * PAIRS)
    return rows.transpose(0, 1, 3, 2, 4).reshape(BLOCK, 2, 2, PAIRS * PAIRS)


def solution(mesh):
    return jax.shard_map(
        on_device,
        mesh=mesh,
        in_specs=(
            P("ka", None, None, "ga"),
            P(),
            P("ka", None),
            P("ka", None),
            P(None, None, None, "ga"),
            P("ga"),
        ),
        out_specs=P("ga", "ka", None, None),
        check_vma=False,
    )
```

```python
import functools

import jax
import jax.numpy as jnp
from jax import lax
from jax.experimental import pallas as pl
from jax.experimental.pallas import tpu as pltpu
from jax.sharding import PartitionSpec as P

MESH = pl.DeviceIdType.MESH
F32, BF16 = jnp.float32, jnp.bfloat16
PAIRS, NG, NQ, NKR, WIDTH = 64, 1024, 8, 128, 256
CHUNKS = 8
RC = PAIRS // CHUNKS
BLOCK = NKR // 4
GROUPS = ((0, 2), (2, 4), (4, 6), (6, 8))
DIRECT = 1
SLABS = 4
SLAB = BLOCK // SLABS
NT = (((1,), (1,)), ((), ()))


def dot(a, b):
    return jnp.dot(a, b, preferred_element_type=F32)


def dot_nt(a, b):
    return lax.dot_general(a, b, NT, preferred_element_type=F32)


def kernel(density, partner, qindex, gshift, screened, coulomb, out,
           D, SG, OH, SH, W, KA, KB, res, xsend, xrecv, keepx, fin, csend, crecv, obuf,
           wsem, out_sem, s_r, z_r, a1_r, a2_r, b1_r, b2_r, x_r, c_r, l_r, osem):
    ka, ga = lax.axis_index("ka"), lax.axis_index("ga")
    y, x, z = ka // 16, (ka // 4) % 4, ka % 4
    half, core = ga // 2, ga % 2
    ym, yp, yo = (y + 3) % 4, (y + 1) % 4, (y + 2) % 4
    xm, xp, xo = (x + 3) % 4, (x + 1) % 4, (x + 2) % 4

    def at(yy, xx, zz):
        return (yy * 16 + xx * 4 + zz, ga)

    mate_ga = half * 2 + (1 - core)
    cross_ga = (1 - half) * 2 + core
    far_ga = (1 - half) * 2 + (1 - core)
    mate, cross = (ka, mate_ga), (ka, cross_ga)
    line = [at(y, x, (z + d) % 4) for d in (1, 2, 3)]
    ring = [at(y, xp, z), at(y, xm, z), at(yp, x, z), at(ym, x, z)]
    ring_b = [ring[2], ring[3], ring[0], ring[1]]
    opposite = [at(y, xo, z), at(yo, x, z)]

    def rc(src, dst, ss, rs, dev):
        return pltpu.make_async_remote_copy(
            src_ref=src, dst_ref=dst, send_sem=ss, recv_sem=rs, device_id=dev, device_id_type=MESH)

    z_s, a1_s, a2_s, b1_s, b2_s, s_s, x_s, c_s = (out_sem.at[i] for i in range(8))

    def got(whole, rs):
        rc(whole, whole, z_s, rs, mate).wait_recv()

    def sent(whole, ss):
        rc(whole, whole, ss, s_r.at[0], mate).wait_send()

    barrier = pltpu.get_barrier_semaphore()
    for peer in line + ring + opposite + [mate, cross]:
        pl.semaphore_signal(barrier, inc=1, device_id=peer, device_id_type=MESH)
    wcopy = pltpu.make_async_copy(screened, W, wsem)
    wcopy.start()

    for h in range(2):
        both = [density[j, h].astype(F32).reshape(CHUNKS, RC, WIDTH) for j in range(2)]
        D[h, :, y, x, z] = jnp.concatenate(both, axis=1).astype(BF16)
    SG[ga] = density[...]
    pl.semaphore_wait(barrier, 11)

    s_parts = [(SG.at[ga], mate), (SG.at[ga], cross), (SG.at[cross_ga], mate)]
    s_land = [SG.at[mate_ga], SG.at[cross_ga], SG.at[far_ga]]

    def s_send(i):
        rc(s_parts[i][0], s_parts[i][0], s_s, s_r.at[i], s_parts[i][1]).start()

    def s_got(i):
        got(s_land[i], s_r.at[i])

    def z_send(g):
        lo, hi = GROUPS[g]
        part = D.at[:, lo:hi, y, x, z]
        for d in range(3):
            rc(part, part, z_s, z_r.at[g], line[d]).start()

    def z_got(g):
        lo, hi = GROUPS[g]
        got(D.at[:, lo:hi, 0, 0, 0:3], z_r.at[g])

    def span(g):
        return pl.ds(GROUPS[g][0], GROUPS[g][1] - GROUPS[g][0])

    def send_all(parts, ss, rs, to):
        for part, dev in zip(parts, to):
            rc(part, part, ss, rs, dev).start()


    def send(name, c):
        if name == "a1":
            w = span(c)
            parts = [D.at[0, w, y, x], D.at[0, w, y, x], D.at[1, w, y, x], D.at[1, w, y, x]]
            send_all(parts, a1_s, a1_r.at[c], ring)
            if c == 0:
                send_all(parts[1:3], z_s, a1_r.at[c], opposite)
        if name == "a2":
            w = span(c)
            parts = [D.at[0, w, y, xm, 0:2], D.at[0, w, y, xp, 2:4], D.at[1, w, ym, x, 0:2], D.at[1, w, yp, x, 2:4]]
            send_all(parts, a2_s, a2_r.at[c], ring)
        if name == "b1":
            parts = [D.at[0, c, y], D.at[0, c, y], D.at[1, c, :, x], D.at[1, c, :, x]]
            send_all(parts, b1_s, b1_r.at[c], ring_b)
            if isinstance(c, int) and c < DIRECT:
                send_all(parts[1:3], b2_s, b1_r.at[c], opposite[::-1])
        if name == "b2":
            parts = [D.at[0, c, ym, 0:2], D.at[0, c, yp, 2:4], D.at[1, c, 0:2, xm], D.at[1, c, 2:4, xp]]
            send_all(parts, b2_s, b2_r.at[c], ring_b)

    def recv(name, c):
        if name == "a1":
            got(D.at[:, span(c), 0, 0:3] if c == 0 else D.at[0, span(c), 0], a1_r.at[c])
        if name == "a2":
            got(D.at[0, span(c), 0, 0:2], a2_r.at[c])
        if name == "b1":
            got(D.at[:, c, 0:3] if isinstance(c, int) and c < DIRECT else D.at[0, c], b1_r.at[c])
        if name == "b2":
            got(D.at[0, c, 0:2], b2_r.at[c])

    def shift_part(b, first):
        rows = pl.ds(pl.multiple_of(b * WIDTH, WIDTH), WIDTH)
        for j in range(2):
            term = dot(SG[b, j].reshape(2 * PAIRS, WIDTH), OH[j, rows, :])
            if first:
                SH[j] = term.astype(BF16)
            else:
                SH[j] = (SH[j].astype(F32) + term).astype(BF16)

    z_send(0)

    def build(t, _):
        rows = pl.ds(pl.multiple_of(t * 64, 64), 64)
        index = lax.broadcasted_iota(jnp.int32, (64, NG), 0) + t * 64
        for j in range(2):
            OH[j, rows, :] = jnp.where(index == gshift[j:j + 1, :], 1.0, 0.0).astype(BF16)
        return 0

    lax.fori_loop(0, NG // 64, build, 0)
    s_send(1)
    s_send(0)
    shift_part(ga, True)

    local = pl.ds(pl.multiple_of(ga * WIDTH, WIDTH), WIDTH)

    def screen(q, _):
        rows = SH[...].reshape(4 * PAIRS, NG)
        by_re, by_im = dot(rows, W[q, 0]), dot(rows, W[q, 1])
        twice = 2.0 * coulomb[...]
        a, b = [], []
        for j in range(2):
            re, im = slice(j * 128, j * 128 + 64), slice(j * 128 + 64, j * 128 + 128)
            own = SH[j, :, local].astype(F32)
            k_re = (twice * own[:64] - (by_re[re] - by_im[im])).astype(BF16)
            k_im = (twice * own[64:] - (by_im[re] + by_re[im])).astype(BF16)
            a += [k_re, k_im]
            b += [k_im, -k_re]
        KA[q] = jnp.concatenate(a, axis=0)
        KB[q] = jnp.concatenate(b, axis=0)
        return 0

    local = pl.ds(pl.multiple_of(ga * WIDTH, WIDTH), WIDTH)

    def screen(q, _):
        rows = SH[...].reshape(4 * PAIRS, NG)
        by_re, by_im = dot(rows, W[q, 0]), dot(rows, W[q, 1])
        twice = 2.0 * coulomb[...]
        a, b = [], []
        for j in range(2):
            re, im = slice(j * 128, j * 128 + 64), slice(j * 128 + 64, j * 128 + 128)
            own = SH[j, :, local].astype(F32)
            k_re = (twice * own[:64] - (by_re[re] - by_im[im])).astype(BF16)
            k_im = (twice * own[64:] - (by_im[re] + by_re[im])).astype(BF16)
            a += [k_re, k_im]
            b += [k_im, -k_re]
        KA[q] = jnp.concatenate(a, axis=0)
        KB[q] = jnp.concatenate(b, axis=0)
        return 0

    z_got(0)
    send("a1", 0)
    s_got(0)
    shift_part(mate_ga, False)
    recv("a1", 0)
    send("b1", 0)
    s_got(1)
    s_send(2)
    send("b1", 1)
    z_send(1)
    z_send(2)
    z_send(3)
    shift_part(cross_ga, False)
    s_got(2)
    shift_part(far_ga, False)
    wcopy.wait()
    lax.fori_loop(0, 5, screen, 0)
    z_got(1)
    send("a1", 1)
    lax.fori_loop(5, NQ, screen, 0)

    def multiply(c, q_lo, q_hi):
        def one(q, _):
            for t in range(4):
                d_re = D[0, c, t].reshape(256, WIDTH)
                d_im = D[1, c, t].reshape(256, WIDTH)
                both = dot_nt(d_re, KA[q]) + dot_nt(d_im, KB[q])
                for k in range(2):
                    res[k, q, t * 32:(t + 1) * 32] = both[:, k * 128:(k + 1) * 128].reshape(32, RC, 128)
            return 0

        lax.fori_loop(q_lo, q_hi, one, 0)

    def pick(block, put):
        def one(i, _):
            col = block * BLOCK + i
            m = partner[col]
            for k in range(2):
                put(i, k, res[k, qindex[k, col], m])
            return 0

        lax.fori_loop(0, BLOCK, one, 0, unroll=8)

    def x_send(c, part):
        rc(xsend.at[c, part], xrecv.at[c, part], x_s, x_r.at[c, part], mate).start()

    def x_got(c, part):
        got(xrecv.at[c, part], x_r.at[c, part])

    def c_send(c):
        x_got(c, 0)
        for part in range(SLABS):
            piece = pl.ds(part * SLAB, SLAB)
            total = keepx[piece] + xrecv[c, 0, piece]
            csend[c, part] = total.reshape(SLAB, 2 * RC, 128).astype(BF16)
            arrived = l_r.at[part] if isinstance(c, int) and c == CHUNKS - 1 else c_r.at[c]
            rc(csend.at[c, part], crecv.at[c, part], c_s, arrived, cross).start()

    def settle(c):
        rows = pl.ds(pl.multiple_of(c * RC, RC), RC)

        def put_far(i, k, v):
            xsend[c, 0, i, k] = v

        def put_mate(i, k, v):
            xsend[c, 1, i, k] = v

        def put_cross(i, k, v):
            keepx[i, k] = v

        def put_own(i, k, v):
            fin[i, k, rows] = v

        pick(far_ga, put_far)
        x_send(c, 0)
        pick(cross_ga, put_cross)
        pick(mate_ga, put_mate)
        x_send(c, 1)
        pick(ga, put_own)

    def finish(c, part):
        rows = pl.ds(pl.multiple_of(c * RC, RC), RC)
        piece = pl.ds(part * SLAB, SLAB)
        theirs = crecv[c, part].astype(F32).reshape(SLAB, 2, RC, 128)
        fin[piece, :, rows] = fin[piece, :, rows] + xrecv[c, 1, piece] + theirs

    def turn(part):
        slot = lax.broadcasted_iota(jnp.int32, (PAIRS, 128), 0)
        pair = lax.broadcasted_iota(jnp.int32, (PAIRS, 128), 1)
        same = (slot % 2 == pair // PAIRS) & (slot // 2 == (pair % PAIRS) // 2)
        chosen = jnp.where(same, 1.0, 0.0).astype(BF16)
        even = pair % 2 == 0

        def one(i, _):
            parts = []
            for k in range(2):
                t = fin[i, k].astype(BF16)
                zero = jnp.zeros_like(t)
                parts += [jnp.where(even, t, zero), jnp.where(even, zero, t)]
            turned = dot_nt(chosen, jnp.concatenate(parts, axis=0)).astype(BF16)
            obuf[i, 0] = turned[:, :128]
            obuf[i, 1] = turned[:, 128:]
            return 0

        lax.fori_loop(part * SLAB, (part + 1) * SLAB, one, 0, unroll=4)

    def o_copy(part):
        piece = pl.ds(part * SLAB, SLAB)
        return pltpu.make_async_copy(obuf.at[piece], out.at[piece], osem.at[part])

    recv("b1", 0)
    multiply(0, 0, 2)
    recv("b1", 1)
    send("b2", 1)
    recv("a1", 1)
    send("a2", 1)
    z_got(2)
    send("a1", 2)
    multiply(0, 2, 6)
    recv("a2", 1)
    send("b1", 2)
    send("b1", 3)
    z_got(3)
    send("a1", 3)
    multiply(0, 6, NQ)
    settle(0)

    recv("b2", 1)
    multiply(1, 0, NQ // 2)
    c_send(0)
    recv("b1", 2)
    send("b2", 2)
    recv("a1", 2)
    send("a2", 2)
    multiply(1, NQ // 2, NQ)
    settle(1)
    recv("a2", 2)
    send("b1", 4)
    recv("a1", 3)
    send("a2", 3)

    def tick(c, _):
        @pl.when(c + 1 < CHUNKS)
        def _():
            recv("b1", c + 1)
            send("b2", c + 1)

        @pl.when(c == 3)
        def _():
            recv("a2", 3)

        @pl.when(c + 3 < CHUNKS)
        def _():
            send("b1", c + 3)

        recv("b2", c)
        multiply(c, 0, NQ // 2)
        c_send(c - 1)
        multiply(c, NQ // 2, NQ)
        settle(c)
        return 0

    lax.fori_loop(2, CHUNKS, tick, 0)
    c_send(CHUNKS - 1)

    def rest(c, _):
        x_got(c, 1)
        return 0

    lax.fori_loop(0, CHUNKS, rest, 0)
    sent(D.at[0, 0], z_s)
    sent(D.at[0, 0:2], a1_s)
    sent(D.at[0, 0, 0:3], a2_s)
    sent(D.at[0], b1_s)
    sent(D.at[0, 0:4], b2_s)
    sent(SG.at[0:3], s_s)
    sent(xsend, x_s)

    def ends(c, _):
        got(crecv.at[c], c_r.at[c])
        for part in range(SLABS):
            finish(c, part)
        return 0

    lax.fori_loop(0, CHUNKS - 1, ends, 0)
    for part in range(SLABS):
        got(crecv.at[CHUNKS - 1, part], l_r.at[part])
        finish(CHUNKS - 1, part)
        turn(part)
        o_copy(part).start()
    sent(csend, c_s)
    for part in range(SLABS):
        o_copy(part).wait()


def move(src, dst):
    dst[...] = src[...]


def on_device(density, partner, qindex, gshift, screened, coulomb):
    vmem = pl.BlockSpec(memory_space=pltpu.VMEM)
    smem = pl.BlockSpec(memory_space=pltpu.SMEM)
    dma = pltpu.SemaphoreType.DMA
    packed = pl.pallas_call(
        kernel,
        out_shape=jax.ShapeDtypeStruct((BLOCK, 2, PAIRS, 128), BF16),
        in_specs=[vmem, smem, smem, vmem, pl.BlockSpec(memory_space=pl.ANY), vmem],
        out_specs=pl.BlockSpec(memory_space=pl.ANY),
        scratch_shapes=[
            pltpu.VMEM((2, CHUNKS, 4, 4, 4, 2 * RC, WIDTH), BF16),
            pltpu.VMEM((4, 2, 2, PAIRS, WIDTH), BF16),
            pltpu.VMEM((2, NG, NG), BF16),
            pltpu.VMEM((2, 2 * PAIRS, NG), BF16),
            pltpu.VMEM((NQ, 2, NG, WIDTH), BF16),
            pltpu.VMEM((NQ, 4 * PAIRS, WIDTH), BF16),
            pltpu.VMEM((NQ, 4 * PAIRS, WIDTH), BF16),
            pltpu.VMEM((2, NQ, NKR, RC, 128), F32),
            pltpu.VMEM((CHUNKS, 2, BLOCK, 2, RC, 128), F32),
            pltpu.VMEM((CHUNKS, 2, BLOCK, 2, RC, 128), F32),
            pltpu.VMEM((BLOCK, 2, RC, 128), F32),
            pltpu.VMEM((BLOCK, 2, PAIRS, 128), F32),
            pltpu.VMEM((CHUNKS, SLABS, SLAB, 2 * RC, 128), BF16),
            pltpu.VMEM((CHUNKS, SLABS, SLAB, 2 * RC, 128), BF16),
            pltpu.VMEM((BLOCK, 2, PAIRS, 128), BF16),
            dma, dma((8,)), dma((3,)), dma((len(GROUPS),)), dma((len(GROUPS),)), dma((len(GROUPS),)),
            dma((CHUNKS,)), dma((CHUNKS,)), dma((CHUNKS, 2)), dma((CHUNKS,)), dma((SLABS,)), dma((SLABS,)),
        ],
        compiler_params=pltpu.CompilerParams(
            collective_id=0, has_side_effects=True, vmem_limit_bytes=56 << 20),
    )(density, partner, qindex, gshift, screened, coulomb.reshape(1, WIDTH))
    packed = pl.pallas_call(
        move,
        out_shape=jax.ShapeDtypeStruct(packed.shape, packed.dtype),
        grid=(2,),
        in_specs=[pl.BlockSpec((BLOCK // 2, 2, PAIRS, 128), lambda i: (i, 0, 0, 0))],
        out_specs=pl.BlockSpec((BLOCK // 2, 2, PAIRS, 128), lambda i: (i, 0, 0, 0)),
    )(packed)
    rows = packed.reshape(BLOCK, 2, PAIRS // 2, 2, 2 * PAIRS)
    return rows.transpose(0, 1, 3, 2, 4).reshape(BLOCK, 2, 2, PAIRS * PAIRS)


def solution(mesh):
    return jax.shard_map(
        on_device,
        mesh=mesh,
        in_specs=(
            P("ka", None, None, "ga"),
            P(),
            P("ka", None),
            P("ka", None),
            P(None, None, None, "ga"),
            P("ga"),
        ),
        out_specs=P("ga", "ka", None, None),
        check_vma=False,
    )
```

```python
import functools

import jax
import jax.numpy as jnp
from jax import lax
from jax.experimental import pallas as pl
from jax.experimental.pallas import tpu as pltpu
from jax.sharding import PartitionSpec as P

MESH = pl.DeviceIdType.MESH
F32, BF16 = jnp.float32, jnp.bfloat16
PAIRS, NG, NQ, NKR, WIDTH = 64, 1024, 8, 128, 256
CHUNKS = 8
RC = PAIRS // CHUNKS
BLOCK = NKR // 4
GROUPS = ((0, 2), (2, 4), (4, 6), (6, 8))
DIRECT = 1
SLABS = 4
SLAB = BLOCK // SLABS
NT = (((1,), (1,)), ((), ()))


def dot(a, b):
    return jnp.dot(a, b, preferred_element_type=F32)


def dot_nt(a, b):
    return lax.dot_general(a, b, NT, preferred_element_type=F32)


def kernel(density, partner, qindex, gshift, screened, coulomb, out,
           D, SG, OH, SH, W, KA, KB, res, xsend, xrecv, keepx, fin, csend, crecv, obuf,
           wsem, out_sem, s_r, z_r, a1_r, a2_r, b1_r, b2_r, x_r, c_r, l_r, osem):
    ka, ga = lax.axis_index("ka"), lax.axis_index("ga")
    y, x, z = ka // 16, (ka // 4) % 4, ka % 4
    half, core = ga // 2, ga % 2
    ym, yp, yo = (y + 3) % 4, (y + 1) % 4, (y + 2) % 4
    xm, xp, xo = (x + 3) % 4, (x + 1) % 4, (x + 2) % 4

    def at(yy, xx, zz):
        return (yy * 16 + xx * 4 + zz, ga)

    mate_ga = half * 2 + (1 - core)
    cross_ga = (1 - half) * 2 + core
    far_ga = (1 - half) * 2 + (1 - core)
    mate, cross = (ka, mate_ga), (ka, cross_ga)
    line = [at(y, x, (z + d) % 4) for d in (1, 2, 3)]
    ring = [at(y, xp, z), at(y, xm, z), at(yp, x, z), at(ym, x, z)]
    ring_b = [ring[2], ring[3], ring[0], ring[1]]
    opposite = [at(y, xo, z), at(yo, x, z)]

    def rc(src, dst, ss, rs, dev):
        return pltpu.make_async_remote_copy(
            src_ref=src, dst_ref=dst, send_sem=ss, recv_sem=rs, device_id=dev, device_id_type=MESH)

    z_s, a1_s, a2_s, b1_s, b2_s, s_s, x_s, c_s = (out_sem.at[i] for i in range(8))

    def got(whole, rs):
        rc(whole, whole, z_s, rs, mate).wait_recv()

    def sent(whole, ss):
        rc(whole, whole, ss, s_r.at[0], mate).wait_send()

    barrier = pltpu.get_barrier_semaphore()
    for peer in line + ring + opposite + [mate, cross]:
        pl.semaphore_signal(barrier, inc=1, device_id=peer, device_id_type=MESH)
    wcopy = pltpu.make_async_copy(screened, W, wsem)
    wcopy.start()

    for h in range(2):
        both = [density[j, h].astype(F32).reshape(CHUNKS, RC, WIDTH) for j in range(2)]
        D[h, :, y, x, z] = jnp.concatenate(both, axis=1).astype(BF16)
    SG[ga] = density[...]
    pl.semaphore_wait(barrier, 11)

    s_parts = [(SG.at[ga], mate), (SG.at[ga], cross), (SG.at[cross_ga], mate)]
    s_land = [SG.at[mate_ga], SG.at[cross_ga], SG.at[far_ga]]

    def s_send(i):
        rc(s_parts[i][0], s_parts[i][0], s_s, s_r.at[i], s_parts[i][1]).start()

    def s_got(i):
        got(s_land[i], s_r.at[i])

    def z_send(g):
        lo, hi = GROUPS[g]
        part = D.at[:, lo:hi, y, x, z]
        for d in range(3):
            rc(part, part, z_s, z_r.at[g], line[d]).start()

    def z_got(g):
        lo, hi = GROUPS[g]
        got(D.at[:, lo:hi, 0, 0, 0:3], z_r.at[g])

    def span(g):
        return pl.ds(GROUPS[g][0], GROUPS[g][1] - GROUPS[g][0])

    def send_all(parts, ss, rs, to):
        for part, dev in zip(parts, to):
            rc(part, part, ss, rs, dev).start()


    def send(name, c):
        if name == "a1":
            w = span(c)
            parts = [D.at[0, w, y, x], D.at[0, w, y, x], D.at[1, w, y, x], D.at[1, w, y, x]]
            send_all(parts, a1_s, a1_r.at[c], ring)
            if c == 0:
                send_all(parts[1:3], z_s, a1_r.at[c], opposite)
        if name == "a2":
            w = span(c)
            parts = [D.at[0, w, y, xm, 0:2], D.at[0, w, y, xp, 2:4], D.at[1, w, ym, x, 0:2], D.at[1, w, yp, x, 2:4]]
            send_all(parts, a2_s, a2_r.at[c], ring)
        if name == "b1":
            parts = [D.at[0, c, y], D.at[0, c, y], D.at[1, c, :, x], D.at[1, c, :, x]]
            send_all(parts, b1_s, b1_r.at[c], ring_b)
            if isinstance(c, int) and c < DIRECT:
                send_all(parts[1:3], b2_s, b1_r.at[c], opposite[::-1])
        if name == "b2":
            parts = [D.at[0, c, ym, 0:2], D.at[0, c, yp, 2:4], D.at[1, c, 0:2, xm], D.at[1, c, 2:4, xp]]
            send_all(parts, b2_s, b2_r.at[c], ring_b)

    def recv(name, c):
        if name == "a1":
            got(D.at[:, span(c), 0, 0:3] if c == 0 else D.at[0, span(c), 0], a1_r.at[c])
        if name == "a2":
            got(D.at[0, span(c), 0, 0:2], a2_r.at[c])
        if name == "b1":
            got(D.at[:, c, 0:3] if isinstance(c, int) and c < DIRECT else D.at[0, c], b1_r.at[c])
        if name == "b2":
            got(D.at[0, c, 0:2], b2_r.at[c])

    def shift_part(b, first):
        rows = pl.ds(pl.multiple_of(b * WIDTH, WIDTH), WIDTH)
        for j in range(2):
            term = dot(SG[b, j].reshape(2 * PAIRS, WIDTH), OH[j, rows, :])
            if first:
                SH[j] = term.astype(BF16)
            else:
                SH[j] = (SH[j].astype(F32) + term).astype(BF16)

    z_send(0)

    def build(t, _):
        rows = pl.ds(pl.multiple_of(t * 64, 64), 64)
        index = lax.broadcasted_iota(jnp.int32, (64, NG), 0) + t * 64
        for j in range(2):
            OH[j, rows, :] = jnp.where(index == gshift[j:j + 1, :], 1.0, 0.0).astype(BF16)
        return 0

    lax.fori_loop(0, NG // 64, build, 0)
    s_send(1)
    s_send(0)
    shift_part(ga, True)

    local = pl.ds(pl.multiple_of(ga * WIDTH, WIDTH), WIDTH)

    def screen(q, _):
        rows = SH[...].reshape(4 * PAIRS, NG)
        by_re, by_im = dot(rows, W[q, 0]), dot(rows, W[q, 1])
        twice = 2.0 * coulomb[...]
        a, b = [], []
        for j in range(2):
            re, im = slice(j * 128, j * 128 + 64), slice(j * 128 + 64, j * 128 + 128)
            own = SH[j, :, local].astype(F32)
            k_re = (twice * own[:64] - (by_re[re] - by_im[im])).astype(BF16)
            k_im = (twice * own[64:] - (by_im[re] + by_re[im])).astype(BF16)
            a += [k_re, k_im]
            b += [k_im, -k_re]
        KA[q] = jnp.concatenate(a, axis=0).T
        KB[q] = jnp.concatenate(b, axis=0).T
        return 0

    local = pl.ds(pl.multiple_of(ga * WIDTH, WIDTH), WIDTH)

    def screen(q, _):
        rows = SH[...].reshape(4 * PAIRS, NG)
        by_re, by_im = dot(rows, W[q, 0]), dot(rows, W[q, 1])
        twice = 2.0 * coulomb[...]
        a, b = [], []
        for j in range(2):
            re, im = slice(j * 128, j * 128 + 64), slice(j * 128 + 64, j * 128 + 128)
            own = SH[j, :, local].astype(F32)
            k_re = (twice * own[:64] - (by_re[re] - by_im[im])).astype(BF16)
            k_im = (twice * own[64:] - (by_im[re] + by_re[im])).astype(BF16)
            a += [k_re, k_im]
            b += [k_im, -k_re]
        KA[q] = jnp.concatenate(a, axis=0).T
        KB[q] = jnp.concatenate(b, axis=0).T
        return 0

    z_got(0)
    send("a1", 0)
    s_got(0)
    shift_part(mate_ga, False)
    recv("a1", 0)
    send("b1", 0)
    s_got(1)
    s_send(2)
    send("b1", 1)
    z_send(1)
    z_send(2)
    z_send(3)
    shift_part(cross_ga, False)
    s_got(2)
    shift_part(far_ga, False)
    wcopy.wait()
    lax.fori_loop(0, 5, screen, 0)
    z_got(1)
    send("a1", 1)
    lax.fori_loop(5, NQ, screen, 0)

    def multiply(c, q_lo, q_hi):
        def one(q, _):
            for t in range(4):
                d_re = D[0, c, t].reshape(256, WIDTH)
                d_im = D[1, c, t].reshape(256, WIDTH)
                both = dot(d_re, KA[q]) + dot(d_im, KB[q])
                for k in range(2):
                    res[k, q, t * 32:(t + 1) * 32] = both[:, k * 128:(k + 1) * 128].reshape(32, RC, 128)
            return 0

        lax.fori_loop(q_lo, q_hi, one, 0)

    def pick(block, put):
        def one(i, _):
            col = block * BLOCK + i
            m = partner[col]
            for k in range(2):
                put(i, k, res[k, qindex[k, col], m])
            return 0

        lax.fori_loop(0, BLOCK, one, 0, unroll=8)

    def x_send(c, part):
        rc(xsend.at[c, part], xrecv.at[c, part], x_s, x_r.at[c, part], mate).start()

    def x_got(c, part):
        got(xrecv.at[c, part], x_r.at[c, part])

    def c_send(c):
        x_got(c, 0)
        for part in range(SLABS):
            piece = pl.ds(part * SLAB, SLAB)
            total = keepx[piece] + xrecv[c, 0, piece]
            csend[c, part] = total.reshape(SLAB, 2 * RC, 128).astype(BF16)
            arrived = l_r.at[part] if isinstance(c, int) and c == CHUNKS - 1 else c_r.at[c]
            rc(csend.at[c, part], crecv.at[c, part], c_s, arrived, cross).start()

    def settle(c):
        rows = pl.ds(pl.multiple_of(c * RC, RC), RC)

        def put_far(i, k, v):
            xsend[c, 0, i, k] = v

        def put_mate(i, k, v):
            xsend[c, 1, i, k] = v

        def put_cross(i, k, v):
            keepx[i, k] = v

        def put_own(i, k, v):
            fin[i, k, rows] = v

        pick(far_ga, put_far)
        x_send(c, 0)
        pick(cross_ga, put_cross)
        pick(mate_ga, put_mate)
        x_send(c, 1)
        pick(ga, put_own)

    def finish(c, part):
        rows = pl.ds(pl.multiple_of(c * RC, RC), RC)
        piece = pl.ds(part * SLAB, SLAB)
        theirs = crecv[c, part].astype(F32).reshape(SLAB, 2, RC, 128)
        fin[piece, :, rows] = fin[piece, :, rows] + xrecv[c, 1, piece] + theirs

    def turn(part):
        slot = lax.broadcasted_iota(jnp.int32, (PAIRS, 128), 0)
        pair = lax.broadcasted_iota(jnp.int32, (PAIRS, 128), 1)
        same = (slot % 2 == pair // PAIRS) & (slot // 2 == (pair % PAIRS) // 2)
        chosen = jnp.where(same, 1.0, 0.0).astype(BF16)
        even = pair % 2 == 0

        def one(i, _):
            parts = []
            for k in range(2):
                t = fin[i, k].astype(BF16)
                zero = jnp.zeros_like(t)
                parts += [jnp.where(even, t, zero), jnp.where(even, zero, t)]
            turned = dot_nt(chosen, jnp.concatenate(parts, axis=0)).astype(BF16)
            obuf[i, 0] = turned[:, :128]
            obuf[i, 1] = turned[:, 128:]
            return 0

        lax.fori_loop(part * SLAB, (part + 1) * SLAB, one, 0, unroll=4)

    def o_copy(part):
        piece = pl.ds(part * SLAB, SLAB)
        return pltpu.make_async_copy(obuf.at[piece], out.at[piece], osem.at[part])

    recv("b1", 0)
    multiply(0, 0, 2)
    recv("b1", 1)
    send("b2", 1)
    recv("a1", 1)
    send("a2", 1)
    z_got(2)
    send("a1", 2)
    multiply(0, 2, 6)
    recv("a2", 1)
    send("b1", 2)
    send("b1", 3)
    z_got(3)
    send("a1", 3)
    multiply(0, 6, NQ)
    settle(0)

    recv("b2", 1)
    multiply(1, 0, NQ // 2)
    c_send(0)
    recv("b1", 2)
    send("b2", 2)
    recv("a1", 2)
    send("a2", 2)
    multiply(1, NQ // 2, NQ)
    settle(1)
    recv("a2", 2)
    send("b1", 4)
    recv("a1", 3)
    send("a2", 3)

    def tick(c, _):
        @pl.when(c + 1 < CHUNKS)
        def _():
            recv("b1", c + 1)
            send("b2", c + 1)

        @pl.when(c == 3)
        def _():
            recv("a2", 3)

        @pl.when(c + 3 < CHUNKS)
        def _():
            send("b1", c + 3)

        recv("b2", c)
        multiply(c, 0, NQ // 2)
        c_send(c - 1)
        multiply(c, NQ // 2, NQ)
        settle(c)
        return 0

    lax.fori_loop(2, CHUNKS, tick, 0)
    c_send(CHUNKS - 1)

    def rest(c, _):
        x_got(c, 1)
        return 0

    lax.fori_loop(0, CHUNKS, rest, 0)
    sent(D.at[0, 0], z_s)
    sent(D.at[0, 0:2], a1_s)
    sent(D.at[0, 0, 0:3], a2_s)
    sent(D.at[0], b1_s)
    sent(D.at[0, 0:4], b2_s)
    sent(SG.at[0:3], s_s)
    sent(xsend, x_s)

    def ends(c, _):
        got(crecv.at[c], c_r.at[c])
        for part in range(SLABS):
            finish(c, part)
        return 0

    lax.fori_loop(0, CHUNKS - 1, ends, 0)
    for part in range(SLABS):
        got(crecv.at[CHUNKS - 1, part], l_r.at[part])
        finish(CHUNKS - 1, part)
        turn(part)
        o_copy(part).start()
    sent(csend, c_s)
    for part in range(SLABS):
        o_copy(part).wait()


def move(src, dst):
    dst[...] = src[...]


def on_device(density, partner, qindex, gshift, screened, coulomb):
    vmem = pl.BlockSpec(memory_space=pltpu.VMEM)
    smem = pl.BlockSpec(memory_space=pltpu.SMEM)
    dma = pltpu.SemaphoreType.DMA
    packed = pl.pallas_call(
        kernel,
        out_shape=jax.ShapeDtypeStruct((BLOCK, 2, PAIRS, 128), BF16),
        in_specs=[vmem, smem, smem, vmem, pl.BlockSpec(memory_space=pl.ANY), vmem],
        out_specs=pl.BlockSpec(memory_space=pl.ANY),
        scratch_shapes=[
            pltpu.VMEM((2, CHUNKS, 4, 4, 4, 2 * RC, WIDTH), BF16),
            pltpu.VMEM((4, 2, 2, PAIRS, WIDTH), BF16),
            pltpu.VMEM((2, NG, NG), BF16),
            pltpu.VMEM((2, 2 * PAIRS, NG), BF16),
            pltpu.VMEM((NQ, 2, NG, WIDTH), BF16),
            pltpu.VMEM((NQ, 4 * PAIRS, WIDTH), BF16),
            pltpu.VMEM((NQ, 4 * PAIRS, WIDTH), BF16),
            pltpu.VMEM((2, NQ, NKR, RC, 128), F32),
            pltpu.VMEM((CHUNKS, 2, BLOCK, 2, RC, 128), F32),
            pltpu.VMEM((CHUNKS, 2, BLOCK, 2, RC, 128), F32),
            pltpu.VMEM((BLOCK, 2, RC, 128), F32),
            pltpu.VMEM((BLOCK, 2, PAIRS, 128), F32),
            pltpu.VMEM((CHUNKS, SLABS, SLAB, 2 * RC, 128), BF16),
            pltpu.VMEM((CHUNKS, SLABS, SLAB, 2 * RC, 128), BF16),
            pltpu.VMEM((BLOCK, 2, PAIRS, 128), BF16),
            dma, dma((8,)), dma((3,)), dma((len(GROUPS),)), dma((len(GROUPS),)), dma((len(GROUPS),)),
            dma((CHUNKS,)), dma((CHUNKS,)), dma((CHUNKS, 2)), dma((CHUNKS,)), dma((SLABS,)), dma((SLABS,)),
        ],
        compiler_params=pltpu.CompilerParams(
            collective_id=0, has_side_effects=True, vmem_limit_bytes=56 << 20),
    )(density, partner, qindex, gshift, screened, coulomb.reshape(1, WIDTH))
    packed = pl.pallas_call(
        move,
        out_shape=jax.ShapeDtypeStruct(packed.shape, packed.dtype),
        grid=(2,),
        in_specs=[pl.BlockSpec((BLOCK // 2, 2, PAIRS, 128), lambda i: (i, 0, 0, 0))],
        out_specs=pl.BlockSpec((BLOCK // 2, 2, PAIRS, 128), lambda i: (i, 0, 0, 0)),
    )(packed)
    rows = packed.reshape(BLOCK, 2, PAIRS // 2, 2, 2 * PAIRS)
    return rows.transpose(0, 1, 3, 2, 4).reshape(BLOCK, 2, 2, PAIRS * PAIRS)


def solution(mesh):
    return jax.shard_map(
        on_device,
        mesh=mesh,
        in_specs=(
            P("ka", None, None, "ga"),
            P(),
            P("ka", None),
            P("ka", None),
            P(None, None, None, "ga"),
            P("ga"),
        ),
        out_specs=P("ga", "ka", None, None),
        check_vma=False,
    )
```
